128 devices in a mesh: row: 8 (over z_hi, x), col: 16 (over y, z_lo, core).
Axes of the slice: x: 4, y: 4, z: 4 (z_hi: 2, z_lo: 2; z = z_hi * 2 + z_lo), core: 2. Of those that a mesh axis runs over, the one named last changes fastest.
Arguments:
- pattern: int32 [32, 32], replicated, may hold values from 0 to 1, as said below
- matrix: bfloat16 [4096, 4096], P('row', 'col'), as said below
Outputs:
- sign_estimate: float32 [4096, 4096], P('row', 'col')
The draws below stay inside these ranges and needn't reach their ends.
Inputs may be any that keep to these rules, and one draw needn't show every extreme that they name: pattern is symmetric, its diagonal is 1, a kept block joins cells at squared distance 5 or less, no block row keeps more than 26 blocks, and some block row keeps exactly 26. matrix is symmetric and zero in every block where pattern is 0.
All inputs are finite; a program needn't handle non-finite values.
Results may differ from the reference program's by a relative error of at most 0.027.
Values may be sent and summed in bfloat16 or wider, within the bound.
A program may use at most 64 MiB of HBM per device.

```python
import jax
import jax.numpy as jnp
from jax import lax

BLOCK = 128
ITERS = 2
NB = 32
ORDER = 4096


def shared_pattern(key):
    index = jnp.arange(NB, dtype=jnp.int32)
    cell_x = index // 16
    cell_y = index // 4 % 4
    cell_z = index % 4
    delta_x = cell_x[:, None] - cell_x[None, :]
    delta_y = cell_y[:, None] - cell_y[None, :]
    delta_z = cell_z[:, None] - cell_z[None, :]
    spacing = delta_x * delta_x + delta_y * delta_y + delta_z * delta_z
    layers = NB // 16
    anchor = jnp.minimum(1, layers - 1) * 16 + 5
    limit = 20 + 60 * (cell_x[:, None] + cell_x[None, :]) // (2 * layers)
    rolled = jax.random.randint(key, (NB, NB), 0, 100)
    upper = (rolled < limit) & (index[:, None] < index[None, :])
    picked = upper | upper.T
    touches = (index[:, None] == anchor) | (index[None, :] == anchor)
    kept = (spacing <= 5) & ((spacing <= 2) | picked | touches)
    return kept.astype(jnp.int32)


def draw_pattern(key, part):
    return shared_pattern(key)


def draw_matrix(key, part):
    kept = shared_pattern(key)
    key = jax.random.fold_in(key, 7)
    values = jax.random.normal(key, (ORDER, ORDER), jnp.float32)
    symmetric = (values + values.T) * 0.70710678
    expanded = jnp.repeat(jnp.repeat(kept.astype(jnp.float32), BLOCK, axis=0), BLOCK, axis=1)
    return (symmetric * expanded).astype(jnp.bfloat16)


def setup_inputs(seed: int = 0) -> dict:
    seeds = jax.random.split(jax.random.key(seed), 3)
    return {
        "pattern": draw_pattern(jax.random.fold_in(seeds[2], 71), 0),
        "matrix": draw_matrix(jax.random.fold_in(seeds[2], 71), 0),
    }


def reference(pattern, matrix):
    expanded = jnp.repeat(jnp.repeat(pattern.astype(jnp.float32), BLOCK, axis=0), BLOCK, axis=1)
    scale = 1.0 / (3.0 * ORDER)
    current = matrix
    for section in range(ITERS):
        widened = current.astype(jnp.float32)
        square = (jnp.dot(widened, widened, precision=lax.Precision.HIGHEST) * expanded * scale).astype(jnp.bfloat16)
        cube = jnp.dot(widened, square.astype(jnp.float32), precision=lax.Precision.HIGHEST)
        updated = expanded * (1.5 * widened - 0.5 * cube)
        if section + 1 < ITERS:
            current = updated.astype(jnp.bfloat16)
        else:
            current = updated
    return current
```

```python
import jax
import jax.numpy as jnp
from jax import lax
from jax.experimental import pallas as pl
from jax.experimental.pallas import tpu as pltpu
from jax.sharding import PartitionSpec as P

MESH = pl.DeviceIdType.MESH
BLOCK = 128
ROWS, COLS = 512, 256
HALF = ROWS // 2
RING = 4


class Gather:
    def __init__(self, buf, place, device, ring, plane, send, recv):
        self.buf, self.place, self.device = buf, place, device
        self.ring, self.plane = ring, plane
        self.send, self.recv = send, recv

    def copy(self, i):
        half, side, plane, hops = {
            0: (0, 1, 0, 0), 1: (1, 1, 0, 0), 2: (0, -1, 0, 0), 3: (1, -1, 0, 0), 4: (0, 0, 0, 0), 5: (1, 0, 0, 0),
            6: (0, 1, 0, 1), 7: (1, -1, 0, 1),
            8: (0, 1, 1, 0), 9: (1, 1, 1, 0), 10: (0, -1, 1, 0), 11: (1, -1, 1, 0),
            12: (0, 1, 1, 1), 13: (1, -1, 1, 1),
        }[i]
        me, p = self.ring, self.plane
        whose = (lax.rem(me - side * hops + RING, RING), p if plane == 0 else 1 - p)
        target = (lax.rem(me + side + RING, RING), p if side else 1 - p)
        ref = self.buf.at[self.place(*whose), pl.ds(half * HALF, HALF)]
        return pltpu.make_async_remote_copy(
            src_ref=ref, dst_ref=ref, send_sem=self.send.at[i], recv_sem=self.recv.at[i],
            device_id=self.device(*target), device_id_type=MESH,
        )

    def arrived(self, i):
        self.copy(i).wait_recv()

    def own(self):
        for i in (0, 3, 4, 2, 1, 5):
            self.copy(i).start()

    def sent(self):
        for i in range(14):
            self.copy(i).wait_send()


STEPS = (((0,), (6,)), ((3,), (7,)), ((4,), (8, 10)), ((5,), (11, 9)), ((8,), (12,)), ((11,), (13,)))
REST = (1, 2, 6, 7, 9, 10, 12, 13)
WHOLE = {1: (-1, 0), 2: (1, 0), 5: (0, 1), 7: (2, 0), 9: (-1, 1), 10: (1, 1), 13: (2, 1)}


def kernel(pattern_ref, y_ref, out_ref, rows, cols, squares, total, send, recv, pair_send, pair_recv):
    row = lax.axis_index("row")
    col = lax.axis_index("col")
    x, z_hi = lax.rem(row, 4), row // 4
    y, z_lo, core = col // 4, lax.rem(col // 2, 2), lax.rem(col, 2)

    def in_row(y_, z_):
        return row, y_ * 4 + z_ * 2 + core

    def in_col(x_, z_):
        return z_ * 4 + x_, col

    sibling = (row, col + 1 - 2 * core)
    barrier = pltpu.get_barrier_semaphore()
    partners = [sibling, in_row(y, 1 - z_lo), in_col(x, 1 - z_hi)]
    for side in (1, 3):
        partners += [in_row(lax.rem(y + side, 4), z_lo), in_col(lax.rem(x + side, 4), z_hi)]
    for partner in partners:
        pl.semaphore_signal(barrier, inc=1, device_id=partner, device_id_type=MESH)
    rows[0, col] = y_ref[...]
    cols[0, row] = y_ref[...]
    pl.semaphore_wait(barrier, len(partners))

    def masked(blocks, store):
        for i in range(ROWS // BLOCK):
            for j in range(COLS // BLOCK):
                keep = pattern_ref[row * 4 + i, col * 2 + j].astype(jnp.float32)
                at = (pl.ds(i * BLOCK, BLOCK), pl.ds(j * BLOCK, BLOCK))
                store(at, keep * blocks(at))

    def product(left, right):
        total[...] = jnp.zeros_like(total)

        def body(k, _):
            part = jnp.dot(left[2 * k], right[k, 0:COLS], preferred_element_type=jnp.float32)
            part += jnp.dot(left[2 * k + 1], right[k, COLS : 2 * COLS], preferred_element_type=jnp.float32)
            total[...] += part
            return 0

        lax.fori_loop(0, 8, body, 0)

    for step in range(2):
        y_rows, y_cols, square = rows.at[step], cols.at[step], squares.at[step]
        by_row = Gather(y_rows, lambda y_, z_: y_ * 4 + z_ * 2 + core, in_row, y, z_lo, send.at[3 * step], recv.at[3 * step])
        by_col = Gather(y_cols, lambda x_, z_: z_ * 4 + x_, in_col, x, z_hi, send.at[3 * step + 1], recv.at[3 * step + 1])

        def share(n, y_, z_):
            ref = y_rows.at[y_ * 4 + z_ * 2 + core]
            return pltpu.make_async_remote_copy(
                src_ref=ref, dst_ref=ref, send_sem=pair_send.at[step, n], recv_sem=pair_recv.at[step, n],
                device_id=sibling, device_id_type=MESH,
            )

        shares = [share(0, y, z_lo)]
        by_row.own()
        by_col.own()
        shares[0].start()
        for waits, starts in STEPS:
            for g in (by_row, by_col):
                for i in waits:
                    g.arrived(i)
                for i in starts:
                    g.copy(i).start()
            if waits == (5,):
                shares.append(share(1, y, 1 - z_lo))
                shares[-1].start()
        for i in REST:
            by_row.arrived(i)
            by_col.arrived(i)
            if i in WHOLE:
                offset, other = WHOLE[i]
                shares.append(share(len(shares), lax.rem(y + offset + 4, 4), 1 - z_lo if other else z_lo))
                shares[-1].start()
        for s in shares:
            s.wait_recv()
        product(y_rows, y_cols)
        scale = 1.0 / (3.0 * 4096)

        def store_square(at, value):
            square[row, at[0], at[1]] = value.astype(jnp.bfloat16)

        masked(lambda at: total[at] * scale, store_square)
        by_square = Gather(square, lambda x_, z_: z_ * 4 + x_, in_col, x, z_hi, send.at[3 * step + 2], recv.at[3 * step + 2])
        by_square.own()
        for waits, starts in STEPS:
            for i in waits:
                by_square.arrived(i)
            for i in starts:
                by_square.copy(i).start()
        for i in REST:
            by_square.arrived(i)
        product(y_rows, square)

        def updated(at):
            return 1.5 * y_rows[col, at[0], at[1]].astype(jnp.float32) - 0.5 * total[at]

        if step == 0:
            def store_next(at, value):
                rows[1, col, at[0], at[1]] = value.astype(jnp.bfloat16)
                cols[1, row, at[0], at[1]] = value.astype(jnp.bfloat16)

            masked(updated, store_next)
        else:
            def store_out(at, value):
                out_ref[at] = value

            masked(updated, store_out)
        by_row.sent()
        by_col.sent()
        by_square.sent()
        for s in shares:
            s.wait_send()


def shards(pattern, matrix):
    return pl.pallas_call(
        kernel,
        name="sign_steps",
        out_shape=jax.ShapeDtypeStruct((ROWS, COLS), jnp.float32),
        in_specs=[pl.BlockSpec(memory_space=pltpu.SMEM), pl.BlockSpec(memory_space=pltpu.VMEM)],
        out_specs=pl.BlockSpec(memory_space=pltpu.VMEM),
        scratch_shapes=[
            pltpu.VMEM((2, 16, ROWS, COLS), jnp.bfloat16),
            pltpu.VMEM((2, 8, ROWS, COLS), jnp.bfloat16),
            pltpu.VMEM((2, 8, ROWS, COLS), jnp.bfloat16),
            pltpu.VMEM((ROWS, COLS), jnp.float32),
            pltpu.SemaphoreType.DMA((6, 14)),
            pltpu.SemaphoreType.DMA((6, 14)),
            pltpu.SemaphoreType.DMA((2, 8)),
            pltpu.SemaphoreType.DMA((2, 8)),
        ],
        compiler_params=pltpu.CompilerParams(collective_id=0, has_side_effects=True, vmem_limit_bytes=40 << 20),
        cost_estimate=pl.CostEstimate(flops=4 * 2 * 512 * 256 * 4096, bytes_accessed=1 << 20, transcendentals=0),
    )(pattern, matrix)


def solution(mesh):
    in_specs = (P(), P("row", "col"))
    return jax.shard_map(shards, mesh=mesh, in_specs=in_specs, out_specs=P("row", "col"), check_vma=False)
```

```python
import jax
import jax.numpy as jnp
from jax import lax
from jax.experimental import pallas as pl
from jax.experimental.pallas import tpu as pltpu
from jax.sharding import PartitionSpec as P

MESH = pl.DeviceIdType.MESH
BLOCK = 128
ROWS, COLS = 512, 256
RING = 4
F32 = jnp.float32

COPIES = (
    (0, 1, 0, 0), (1, 1, 0, 0), (0, -1, 0, 0), (1, -1, 0, 0), (0, 0, 0, 0), (1, 0, 0, 0),
    (0, 1, 0, 1), (1, -1, 0, 1),
    (0, 1, 1, 0), (1, 1, 1, 0), (0, -1, 1, 0), (1, -1, 1, 0),
    (0, 1, 1, 1), (1, -1, 1, 1),
)
OWN = (0, 3, 4, 5, 2, 1)
RELAYS = ((0, (6,)), (3, (7,)), (4, (8, 10)), (5, (11, 9)), (8, (12,)), (11, (13,)))
NEAR = (1, 2, 6, 7)
FAR = (9, 10, 12, 13)
WHOLE = {5: (0, 1), 1: (-1, 0), 2: (1, 0), 7: (2, 0), 9: (-1, 1), 10: (1, 1), 13: (2, 1)}


def ring(i):
    return lax.rem(i + RING, RING)


def reach(cell, other):
    dx = lax.max(cell[0] - other[0], other[0] - cell[0])
    dy = lax.max(cell[1] - other[1], other[1] - cell[1])
    return jnp.where(dy == 3, -1, lax.min(2, 3 - dx - dy))


def run(width, inner, core):
    if not inner:
        return core * (3 - width), width + 1
    return ((core + 1, 1), (core, 3), (0, 4))[width]


def when_reach(r, action):
    for width in range(3):
        pl.when(r == width)(lambda width=width: action(width))


class Gather:
    def __init__(self, buf, place, device, cell, fixed, core, me, plane, send, recv):
        self.buf, self.place, self.device, self.cell = buf, place, device, cell
        self.fixed, self.core, self.me, self.plane = fixed, core, me, plane
        self.send, self.recv = send, recv

    def each(self, i, arriving, action):
        inner, side, other, hops = COPIES[i]
        if side:
            owner = (ring(self.me - side * (hops + arriving)), 1 - self.plane if other else self.plane)
        else:
            owner = (self.me, 1 - self.plane if arriving else self.plane)
        target = (ring(self.me + side), self.plane if side else 1 - self.plane)
        j = 1 - self.core if inner else self.core

        def act(width):
            low, count = run(width, inner, self.core)
            ref = self.buf.at[self.place(*owner), j, pl.ds(low * BLOCK, count * BLOCK)]
            action(pltpu.make_async_remote_copy(
                src_ref=ref, dst_ref=ref, send_sem=self.send.at[i], recv_sem=self.recv.at[i],
                device_id=self.device(*target), device_id_type=MESH,
            ))

        when_reach(reach(self.cell(*owner), self.fixed), act)

    def start(self, *numbers):
        for i in numbers:
            self.each(i, 0, lambda copy: copy.start())

    def arrived(self, i):
        self.each(i, 1, lambda copy: copy.wait_recv())

    def sent(self):
        for i in range(len(COPIES)):
            self.each(i, 0, lambda copy: copy.wait_send())


def kernel(pattern_hbm, y_hbm, out_ref, pattern, rows, cols, squares, total, local, send, recv, pair_send, pair_recv):
    row = lax.axis_index("row")
    col = lax.axis_index("col")
    x, z_hi = lax.rem(row, 4), row // 4
    y, z_lo, core = col // 4, lax.rem(col // 2, 2), lax.rem(col, 2)

    def in_row(y_, z_):
        return row, y_ * 4 + z_ * 2 + core

    def in_col(x_, z_):
        return z_ * 4 + x_, col

    def row_place(y_, z_):
        return y_ * 4 + z_ * 2 + core

    def col_place(x_, z_):
        return z_ * 4 + x_

    def row_cell(y_, z_):
        return y_ // 2, lax.rem(y_, 2) * 2 + z_

    def col_cell(x_, z_):
        return z_, x_

    p, q = col_cell(x, z_hi), row_cell(y, z_lo)
    sibling = (row, col + 1 - 2 * core)
    barrier = pltpu.get_barrier_semaphore()
    partners = [sibling, in_row(y, 1 - z_lo), in_col(x, 1 - z_hi)]
    for side in (1, 3):
        partners += [in_row(ring(y + side), z_lo), in_col(ring(x + side), z_hi)]
    for partner in partners:
        pl.semaphore_signal(barrier, inc=1, device_id=partner, device_id_type=MESH)
    loads = [pltpu.make_async_copy(pattern_hbm, pattern, local.at[4])]
    for j in range(2):
        half = y_hbm.at[:, pl.ds(j * BLOCK, BLOCK)]
        loads.append(pltpu.make_async_copy(half, rows.at[0, col, j], local.at[j]))
        loads.append(pltpu.make_async_copy(half, cols.at[0, row, j], local.at[2 + j]))
    for load in loads:
        load.start()
    for load in loads:
        load.wait()
    pl.semaphore_wait(barrier, len(partners))

    def clear(refs, place, cell, fixed, side):
        def wipe(j, low, count):
            for ref in refs:
                for step in range(2):
                    ref[step, place, j, pl.ds(low * BLOCK, count * BLOCK)] = jnp.zeros((count * BLOCK, BLOCK), jnp.bfloat16)

        r = reach(cell, fixed)

        @pl.when(r == -1)
        def _():
            for j in range(2):
                wipe(j, 0, 4)

        def act(width):
            wipe(side, (1 - side) * (width + 1), 3 - width)
            if width == 1:
                wipe(1 - side, (1 - side) * 3, 1)
            if width == 0:
                for low in (0, 2 - side, 3):
                    wipe(1 - side, low, 1)

        when_reach(r, act)

    def clear_all():
        def at_row(s, _):
            clear((rows,), s, row_cell(s // 4, lax.rem(s // 2, 2)), p, lax.rem(s, 2))
            return 0

        def at_col(s, _):
            clear((cols, squares), s, col_cell(lax.rem(s, 4), s // 4), q, core)
            return 0

        lax.fori_loop(0, 16, at_row, 0)
        lax.fori_loop(0, 8, at_col, 0)

    def product(left, right, m, places):
        at = pl.ds(m * COLS, COLS)
        terms = []
        for k in places:
            for c in range(2):
                l = jnp.concatenate([left[2 * k + c, j, at] for j in range(2)], axis=1)
                r = jnp.concatenate([right[k, j, pl.ds(c * COLS, COLS)] for j in range(2)], axis=1)
                terms.append(jnp.dot(l, r, preferred_element_type=F32))
        return sum(terms)

    def masked(m, value, store):
        for i in range(2):
            for j in range(2):
                keep = pattern[row * 4 + 2 * m + i, col * 2 + j].astype(F32)
                block = value(pl.ds((2 * m + i) * BLOCK, BLOCK), i, j)
                store(pl.ds((2 * m + i) * BLOCK, BLOCK), j, keep * block)

    def one_step(step, _):
        y_rows, y_cols, square = rows.at[step], cols.at[step], squares.at[step]
        n = 3 * step
        by_row = Gather(y_rows, row_place, in_row, row_cell, p, core, y, z_lo, send.at[n], recv.at[n])
        by_col = Gather(y_cols, col_place, in_col, col_cell, q, core, x, z_hi, send.at[n + 1], recv.at[n + 1])
        by_square = Gather(square, col_place, in_col, col_cell, q, core, x, z_hi, send.at[n + 2], recv.at[n + 2])
        shared = []

        def share(number, y_, z_, side, action):
            whose = 1 - core if side else core

            def act(width):
                for inner in range(2):
                    low, count = run(width, inner, whose)
                    j = 1 - whose if inner else whose
                    ref = y_rows.at[y_ * 4 + z_ * 2 + whose, j, pl.ds(low * BLOCK, count * BLOCK)]
                    action(pltpu.make_async_remote_copy(
                        src_ref=ref, dst_ref=ref, send_sem=pair_send.at[step, number, inner],
                        recv_sem=pair_recv.at[step, number, inner], device_id=sibling, device_id_type=MESH,
                    ))

            when_reach(reach(row_cell(y_, z_), p), act)

        def share_start(y_, z_):
            share(len(shared), y_, z_, 0, lambda copy: copy.start())
            shared.append((y_, z_))

        by_row.start(*OWN)
        by_col.start(*OWN)
        share_start(y, z_lo)
        pl.when(step == 0)(clear_all)
        for i, then in RELAYS:
            for g in (by_row, by_col):
                g.arrived(i)
                g.start(*then)
            if i in WHOLE:
                share_start(y, 1 - z_lo)
        for i in NEAR + FAR:
            by_row.arrived(i)
            if i in WHOLE:
                offset, other = WHOLE[i]
                share_start(ring(y + offset), 1 - z_lo if other else z_lo)
        for i in NEAR + FAR:
            by_col.arrived(i)
        for number, (y_, z_) in enumerate(shared):
            share(number, y_, z_, 1, lambda copy: copy.wait_recv())
        scale = 1.0 / (3.0 * 4096)
        for m in range(2):
            full = product(y_rows, y_cols, m, range(8))

            def store_square(at, j, block):
                square[row, j, at] = block.astype(jnp.bfloat16)

            masked(m, lambda at, i, j: full[i * BLOCK : (i + 1) * BLOCK, j * BLOCK : (j + 1) * BLOCK] * scale, store_square)
        by_square.start(*OWN)
        for i, then in RELAYS:
            by_square.arrived(i)
            by_square.start(*then)
        for i in NEAR:
            by_square.arrived(i)
        for m in range(2):
            total[pl.ds(m * COLS, COLS)] = product(y_rows, square, m, [z_hi * 4 + k for k in range(4)])
        for i in FAR:
            by_square.arrived(i)
        for m in range(2):
            full = total[pl.ds(m * COLS, COLS)] + product(y_rows, square, m, [(1 - z_hi) * 4 + k for k in range(4)])

            def updated(at, i, j):
                cube = full[i * BLOCK : (i + 1) * BLOCK, j * BLOCK : (j + 1) * BLOCK]
                return 1.5 * y_rows[col, j, at].astype(F32) - 0.5 * cube

            def store_next(at, j, block):
                @pl.when(step == 0)
                def _():
                    rows[1, col, j, at] = block.astype(jnp.bfloat16)
                    cols[1, row, j, at] = block.astype(jnp.bfloat16)

                @pl.when(step == 1)
                def _():
                    out_ref[at, pl.ds(j * BLOCK, BLOCK)] = block

            masked(m, updated, store_next)
        for g in (by_row, by_col, by_square):
            g.sent()
        for number, (y_, z_) in enumerate(shared):
            share(number, y_, z_, 0, lambda copy: copy.wait_send())
        return 0

    lax.fori_loop(0, 2, one_step, 0)


def shards(pattern, matrix):
    return pl.pallas_call(
        kernel,
        name="sign_steps",
        out_shape=jax.ShapeDtypeStruct((ROWS, COLS), F32),
        in_specs=[pl.BlockSpec(memory_space=pl.ANY), pl.BlockSpec(memory_space=pl.ANY)],
        out_specs=pl.BlockSpec(memory_space=pltpu.VMEM),
        scratch_shapes=[
            pltpu.SMEM((32, 32), jnp.int32),
            pltpu.VMEM((2, 16, 2, ROWS, BLOCK), jnp.bfloat16),
            pltpu.VMEM((2, 8, 2, ROWS, BLOCK), jnp.bfloat16),
            pltpu.VMEM((2, 8, 2, ROWS, BLOCK), jnp.bfloat16),
            pltpu.VMEM((ROWS, COLS), F32),
            pltpu.SemaphoreType.DMA((5,)),
            pltpu.SemaphoreType.DMA((6, len(COPIES))),
            pltpu.SemaphoreType.DMA((6, len(COPIES))),
            pltpu.SemaphoreType.DMA((2, 8, 2)),
            pltpu.SemaphoreType.DMA((2, 8, 2)),
        ],
        compiler_params=pltpu.CompilerParams(collective_id=0, has_side_effects=True, vmem_limit_bytes=56 << 20),
        cost_estimate=pl.CostEstimate(flops=4 * 2 * 512 * 256 * 4096, bytes_accessed=1 << 20, transcendentals=0),
    )(pattern, matrix)


def solution(mesh):
    in_specs = (P(), P("row", "col"))
    return jax.shard_map(shards, mesh=mesh, in_specs=in_specs, out_specs=P("row", "col"), check_vma=False)
```

```python
import jax
import jax.numpy as jnp
from jax import lax
from jax.experimental import pallas as pl
from jax.experimental.pallas import tpu as pltpu
from jax.sharding import PartitionSpec as P

MESH = pl.DeviceIdType.MESH
BLOCK = 128
ROWS, COLS = 512, 256
RING = 4
F32 = jnp.float32

COPIES = (
    ("up", 1, 0, 0), ("not up", 1, 0, 0), ("not down", -1, 0, 0), ("down", -1, 0, 0), ("up", 0, 0, 0), ("not up", 0, 0, 0),
    ("relay", 1, -1, 0), ("relay down", -1, 1, 0),
    ("up", 1, 0, 1), ("not up", 1, 0, 1), ("not down", -1, 0, 1), ("down", -1, 0, 1),
    ("relay", 1, -1, 1), ("relay down", -1, 1, 1),
)
ACROSS = COPIES[:12] + (("far", 0, 2, 0), ("not far", 0, 2, 0))
SECOND = (1, 2, 9, 10)


def same_halves(me, half):
    return half in ("up", "not down", "relay", "far")


def near_centre(me, half):
    return {
        "up": me < 2, "not up": me >= 2, "down": me >= 2, "not down": me < 2, "relay": (me + 1) // 2 == 1,
        "relay down": (me + 1) // 2 == 1, "far": me >= 2, "not far": me < 2,
    }[half]


AROUND = (COPIES, {0: (6,), 3: (7,), 4: (8,), 5: (11, 9, 10), 8: (12,), 11: (13,)})
OVER = (ACROSS, {0: (6,), 3: (7,), 4: (8, 10), 5: (11, 9), 6: (12,), 7: (13,)})
TILES = {(0, 1): (-1, 0), (2, 3): (1, 0), (4, 5): (0, 1), (6, 7): (2, 0), (8, 9): (-1, 1), (10, 11): (1, 1), (12, 13): (2, 1)}
OWN = ("c4", "c0", "r0", "c3", "r3", "c5", "c1", "r1", "c2", "r2", "r4", "r5")
WAITS = (
    "r0", "c0", "r3", "c3", "c4", "c5", "r1", "r2", "r6", "r7", "r4", "c8", "c11", "r5",
    "r8", "r9", "r10", "r11", "r12", "r13", "c1", "c2", "c6", "c7", "c9", "c10", "c12", "c13",
)
SQUARE_OWN = (4, 0, 3, 5, 1, 2)
SQUARE_WAITS = (0, 3, 4, 5, 6, 7, 1, 2, 8, 9, 10, 11, 12, 13)
ROW_KIND, COL_KIND, SQUARE_KIND = OVER, AROUND, OVER


def ring(i):
    return lax.rem(i + RING, RING)


def reach(cell, other):
    dx = lax.max(cell[0] - other[0], other[0] - cell[0])
    dy = lax.max(cell[1] - other[1], other[1] - cell[1])
    return jnp.where(dy == 3, -1, lax.min(2, 3 - dx - dy))


def run(width, inner, core):
    if not inner:
        return core * (3 - width), width + 1
    return ((core + 1, 1), (core, 3), (0, 4))[width]


def when_reach(r, action):
    for width in range(3):
        pl.when(r == width)(lambda width=width: action(width))


class Gather:
    def __init__(self, buf, place, device, cell, fixed, core, me, plane, send, recv, kind, halves):
        self.copies, self.then = kind
        self.halves = halves
        self.buf, self.place, self.device, self.cell = buf, place, device, cell
        self.fixed, self.core, self.me, self.plane = fixed, core, me, plane
        self.send, self.recv = send, recv

    def each(self, i, arriving, action):
        half, side, offset, other = self.copies[i]
        sender = ring(self.me - side) if arriving and side else self.me
        plane = 1 - self.plane if arriving and not side else self.plane
        owner = (ring(sender + offset), 1 - plane if other else plane)
        target = (ring(self.me + side), self.plane if side else 1 - self.plane)
        outer = self.halves(sender, half)
        r = reach(self.cell(*owner), self.fixed)
        if self.halves is near_centre and i in SECOND:
            r = jnp.where(sender == (3 if side > 0 else 0), -1, r)

        def act(width, inner):
            low, count = run(width, inner, self.core)
            j = 1 - self.core if inner else self.core
            ref = self.buf.at[self.place(*owner), j, pl.ds(low * BLOCK, count * BLOCK)]
            action(pltpu.make_async_remote_copy(
                src_ref=ref, dst_ref=ref, send_sem=self.send.at[i], recv_sem=self.recv.at[i],
                device_id=self.device(*target), device_id_type=MESH,
            ))

        if isinstance(outer, bool):
            when_reach(r, lambda width: act(width, not outer))
        else:
            code = r * 2 + jnp.where(outer, 0, 1)
            for width in range(3):
                for inner in (False, True):
                    pl.when(code == 2 * width + inner)(lambda width=width, inner=inner: act(width, inner))

    def start(self, *numbers):
        for i in numbers:
            self.each(i, 0, lambda copy: copy.start())

    def arrived(self, i):
        self.each(i, 1, lambda copy: copy.wait_recv())
        self.start(*self.then.get(i, ()))

    def sent(self):
        for i in range(len(COPIES)):
            self.each(i, 0, lambda copy: copy.wait_send())


def kernel(pattern_hbm, y_hbm, out_ref, pattern, rows, cols, squares, total, local, send, recv, pair_send, pair_recv):
    row = lax.axis_index("row")
    col = lax.axis_index("col")
    x, z_hi = lax.rem(row, 4), row // 4
    y, z_lo, core = col // 4, lax.rem(col // 2, 2), lax.rem(col, 2)

    def in_row(y_, z_):
        return row, y_ * 4 + z_ * 2 + core

    def in_col(x_, z_):
        return z_ * 4 + x_, col

    def row_place(y_, z_):
        return y_ * 4 + z_ * 2 + core

    def col_place(x_, z_):
        return z_ * 4 + x_

    def row_cell(y_, z_):
        return y_ // 2, lax.rem(y_, 2) * 2 + z_

    def col_cell(x_, z_):
        return z_, x_

    p, q = col_cell(x, z_hi), row_cell(y, z_lo)
    sibling = (row, col + 1 - 2 * core)
    barrier = pltpu.get_barrier_semaphore()
    partners = [sibling, in_row(y, 1 - z_lo), in_col(x, 1 - z_hi)]
    for side in (1, 3):
        partners += [in_row(ring(y + side), z_lo), in_col(ring(x + side), z_hi)]
    for partner in partners:
        pl.semaphore_signal(barrier, inc=1, device_id=partner, device_id_type=MESH)
    loads = [pltpu.make_async_copy(pattern_hbm, pattern, local.at[4])]
    for j in range(2):
        half = y_hbm.at[:, pl.ds(j * BLOCK, BLOCK)]
        loads.append(pltpu.make_async_copy(half, rows.at[0, col, j], local.at[j]))
        loads.append(pltpu.make_async_copy(half, cols.at[0, row, j], local.at[2 + j]))
    for load in loads:
        load.start()
    for load in loads:
        load.wait()
    pl.semaphore_wait(barrier, len(partners))

    def clear(refs, place, cell, fixed, side):
        def wipe(j, low, count):
            for ref in refs:
                for step in range(2):
                    ref[step, place, j, pl.ds(low * BLOCK, count * BLOCK)] = jnp.zeros((count * BLOCK, BLOCK), jnp.bfloat16)

        r = reach(cell, fixed)

        @pl.when(r == -1)
        def _():
            for j in range(2):
                wipe(j, 0, 4)

        def act(width):
            wipe(side, (1 - side) * (width + 1), 3 - width)
            if width == 1:
                wipe(1 - side, (1 - side) * 3, 1)
            if width == 0:
                for low in (0, 2 - side, 3):
                    wipe(1 - side, low, 1)

        when_reach(r, act)
        return wipe

    def clear_all():
        def at_row(s, _):
            clear((rows,), 2 * s + core, row_cell(s // 2, lax.rem(s, 2)), p, core)
            return 0

        def at_col(s, _):
            wipe = clear((cols, squares), s, col_cell(lax.rem(s, 4), s // 4), q, core)
            pl.when(lax.rem(s, 4) + x == 3)(lambda: pl.when(lax.rem(x, 3) == 0)(lambda: wipe(core, 0, 4)))
            return 0

        lax.fori_loop(0, 8, at_row, 0)
        lax.fori_loop(0, 8, at_col, 0)

    def product(left, right, m, places):
        at = pl.ds(m * COLS, COLS)
        terms = []
        for k in places:
            for c in range(2):
                l = jnp.concatenate([left[2 * k + c, j, at] for j in range(2)], axis=1)
                r = jnp.concatenate([right[k, j, pl.ds(c * COLS, COLS)] for j in range(2)], axis=1)
                terms.append(jnp.dot(l, r, preferred_element_type=F32))
        return sum(terms)

    def masked(m, value, store):
        for i in range(2):
            for j in range(2):
                keep = pattern[row * 4 + 2 * m + i, col * 2 + j].astype(F32)
                block = value(pl.ds((2 * m + i) * BLOCK, BLOCK), i, j)
                store(pl.ds((2 * m + i) * BLOCK, BLOCK), j, keep * block)

    def square_gather(step):
        n = 3 * step + 2
        return Gather(squares.at[step], col_place, in_col, col_cell, q, core, x, z_hi, send.at[n], recv.at[n], SQUARE_KIND, near_centre)

    def one_step(step, _):
        y_rows, y_cols, square = rows.at[step], cols.at[step], squares.at[step]
        n = 3 * step
        by_row = Gather(y_rows, row_place, in_row, row_cell, p, core, y, z_lo, send.at[n], recv.at[n], ROW_KIND, same_halves)
        by_col = Gather(y_cols, col_place, in_col, col_cell, q, core, x, z_hi, send.at[n + 1], recv.at[n + 1], COL_KIND, near_centre)
        by_square = square_gather(step)
        shared = []

        def share(number, y_, z_, side):
            ref = y_rows.at[y_ * 4 + z_ * 2 + (1 - core if side else core)]
            return pltpu.make_async_remote_copy(
                src_ref=ref, dst_ref=ref, send_sem=pair_send.at[step, number], recv_sem=pair_recv.at[step, number],
                device_id=sibling, device_id_type=MESH,
            )

        def share_start(y_, z_):
            share(len(shared), y_, z_, 0).start()
            shared.append((y_, z_))

        gathers = {"r": by_row, "c": by_col}
        for name in OWN:
            gathers[name[0]].start(int(name[1:]))
        pl.when(step == 0)(clear_all)
        share_start(y, z_lo)
        here = set()
        for name in WAITS:
            gathers[name[0]].arrived(int(name[1:]))
            if name[0] == "r":
                here.add(int(name[1:]))
                for parts, (offset, other) in TILES.items():
                    if int(name[1:]) in parts and here.issuperset(parts):
                        share_start(ring(y + offset), 1 - z_lo if other else z_lo)
        pl.when(step == 1)(square_gather(0).sent)
        for number, (y_, z_) in enumerate(shared):
            share(number, y_, z_, 1).wait_recv()
        scale = 1.0 / (3.0 * 4096)
        for m in range(2):
            full = product(y_rows, y_cols, m, range(8))

            def store_square(at, j, block):
                square[row, j, at] = block.astype(jnp.bfloat16)

            masked(m, lambda at, i, j: full[i * BLOCK : (i + 1) * BLOCK, j * BLOCK : (j + 1) * BLOCK] * scale, store_square)
        by_square.start(*SQUARE_OWN)
        for i in SQUARE_WAITS[:8]:
            by_square.arrived(i)
        by_row.sent()
        by_col.sent()
        for number, (y_, z_) in enumerate(shared):
            share(number, y_, z_, 0).wait_send()
        for m in range(2):
            total[pl.ds(m * COLS, COLS)] = product(y_rows, square, m, [z_hi * 4 + k for k in range(4)])
        for i in SQUARE_WAITS[8:]:
            by_square.arrived(i)
        for m in range(2):
            full = total[pl.ds(m * COLS, COLS)] + product(y_rows, square, m, [(1 - z_hi) * 4 + k for k in range(4)])

            def updated(at, i, j):
                cube = full[i * BLOCK : (i + 1) * BLOCK, j * BLOCK : (j + 1) * BLOCK]
                return 1.5 * y_rows[col, j, at].astype(F32) - 0.5 * cube

            def store_next(at, j, block):
                @pl.when(step == 0)
                def _():
                    rows[1, col, j, at] = block.astype(jnp.bfloat16)
                    cols[1, row, j, at] = block.astype(jnp.bfloat16)

                @pl.when(step == 1)
                def _():
                    out_ref[at, pl.ds(j * BLOCK, BLOCK)] = block

            masked(m, updated, store_next)
        return 0

    lax.fori_loop(0, 2, one_step, 0)
    square_gather(1).sent()


def shards(pattern, matrix):
    return pl.pallas_call(
        kernel,
        name="sign_steps",
        out_shape=jax.ShapeDtypeStruct((ROWS, COLS), F32),
        in_specs=[pl.BlockSpec(memory_space=pl.ANY)] * 2,
        out_specs=pl.BlockSpec(memory_space=pltpu.VMEM),
        scratch_shapes=[
            pltpu.SMEM((32, 32), jnp.int32),
            pltpu.VMEM((2, 16, 2, ROWS, BLOCK), jnp.bfloat16),
            pltpu.VMEM((2, 8, 2, ROWS, BLOCK), jnp.bfloat16),
            pltpu.VMEM((2, 8, 2, ROWS, BLOCK), jnp.bfloat16),
            pltpu.VMEM((ROWS, COLS), F32),
            pltpu.SemaphoreType.DMA((5,)),
            pltpu.SemaphoreType.DMA((6, len(COPIES))),
            pltpu.SemaphoreType.DMA((6, len(COPIES))),
            pltpu.SemaphoreType.DMA((2, 8)),
            pltpu.SemaphoreType.DMA((2, 8)),
        ],
        compiler_params=pltpu.CompilerParams(collective_id=0, has_side_effects=True, vmem_limit_bytes=56 << 20),
        cost_estimate=pl.CostEstimate(flops=4 * 2 * 512 * 256 * 4096, bytes_accessed=1 << 20, transcendentals=0),
    )(pattern, matrix)


def solution(mesh):
    in_specs = (P(), P("row", "col"))
    return jax.shard_map(shards, mesh=mesh, in_specs=in_specs, out_specs=P("row", "col"), check_vma=False)
```

```python
import jax
import jax.numpy as jnp
from jax import lax
from jax.experimental import pallas as pl
from jax.experimental.pallas import tpu as pltpu
from jax.sharding import PartitionSpec as P

MESH = pl.DeviceIdType.MESH
BLOCK = 128
ROWS, COLS = 512, 256
RING = 4
F32 = jnp.float32

COPIES = (
    ("up", 1, 0, 0), ("not up", 1, 0, 0), ("not down", -1, 0, 0), ("down", -1, 0, 0), ("up", 0, 0, 0), ("not up", 0, 0, 0),
    ("relay", 1, -1, 0), ("relay down", -1, 1, 0),
    ("up", 1, 0, 1), ("not up", 1, 0, 1), ("not down", -1, 0, 1), ("down", -1, 0, 1),
    ("relay", 1, -1, 1), ("relay down", -1, 1, 1),
)
ACROSS = COPIES[:12] + (("far", 0, 2, 0), ("not far", 0, 2, 0))
SECOND = (1, 2, 9, 10)


def same_halves(me, half):
    return half in ("up", "not down", "relay", "far")


def near_centre(me, half):
    return {
        "up": me < 2, "not up": me >= 2, "down": me >= 2, "not down": me < 2, "relay": (me + 1) // 2 == 1,
        "relay down": (me + 1) // 2 == 1, "far": me >= 2, "not far": me < 2,
    }[half]


AROUND = (COPIES, {0: (6,), 3: (7,), 4: (8,), 5: (11, 9, 10), 8: (12,), 11: (13,)})
OVER = (ACROSS, {0: (6,), 3: (7,), 4: (8, 10), 5: (11, 9), 6: (12,), 7: (13,)})
TILES = {(0, 1): (-1, 0), (2, 3): (1, 0), (4, 5): (0, 1), (6, 7): (2, 0), (8, 9): (-1, 1), (10, 11): (1, 1), (12, 13): (2, 1)}
OWN = ("c4", "c0", "r0", "c3", "r3", "c5", "c1", "r1", "c2", "r2", "r4", "r5")
WAITS = (
    "r0", "c0", "r3", "c3", "c4", "c5", "r1", "r2", "r6", "r7", "r4", "c8", "c11", "r5",
    "r8", "r9", "r10", "r11", "r12", "r13", "c1", "c2", "c6", "c7", "c9", "c10", "c12", "c13",
)
SQUARE_OWN = (4, 0, 3, 5, 1, 2)
SQUARE_WAITS = (0, 3, 4, 5, 6, 7, 1, 2, 8, 9, 10, 11, 12, 13)
ROW_KIND, COL_KIND, SQUARE_KIND = OVER, AROUND, OVER


def ring(i):
    return lax.rem(i + RING, RING)


def reach(cell, other):
    dx = lax.max(cell[0] - other[0], other[0] - cell[0])
    dy = lax.max(cell[1] - other[1], other[1] - cell[1])
    return jnp.where(dy == 3, -1, lax.min(2, 3 - dx - dy))


def run(width, inner, core):
    if not inner:
        return core * (3 - width), width + 1
    return ((core + 1, 1), (core, 3), (0, 4))[width]


def when_reach(r, action):
    for width in range(3):
        pl.when(r == width)(lambda width=width: action(width))


class Gather:
    def __init__(self, buf, place, device, cell, fixed, core, me, plane, send, recv, kind, halves):
        self.copies, self.then = kind
        self.halves = halves
        self.buf, self.place, self.device, self.cell = buf, place, device, cell
        self.fixed, self.core, self.me, self.plane = fixed, core, me, plane
        self.send, self.recv = send, recv

    def each(self, i, arriving, action):
        half, side, offset, other = self.copies[i]
        sender = ring(self.me - side) if arriving and side else self.me
        plane = 1 - self.plane if arriving and not side else self.plane
        owner = (ring(sender + offset), 1 - plane if other else plane)
        target = (ring(self.me + side), self.plane if side else 1 - self.plane)
        outer = self.halves(sender, half)
        r = reach(self.cell(*owner), self.fixed)
        if self.halves is near_centre and i in SECOND:
            r = jnp.where(sender == (3 if side > 0 else 0), -1, r)

        def act(width, inner):
            low, count = run(width, inner, self.core)
            j = 1 - self.core if inner else self.core
            ref = self.buf.at[self.place(*owner), j, pl.ds(low * BLOCK, count * BLOCK)]
            action(pltpu.make_async_remote_copy(
                src_ref=ref, dst_ref=ref, send_sem=self.send.at[i], recv_sem=self.recv.at[i],
                device_id=self.device(*target), device_id_type=MESH,
            ))

        if isinstance(outer, bool):
            when_reach(r, lambda width: act(width, not outer))
        else:
            code = r * 2 + jnp.where(outer, 0, 1)
            for width in range(3):
                for inner in (False, True):
                    pl.when(code == 2 * width + inner)(lambda width=width, inner=inner: act(width, inner))

    def start(self, *numbers):
        for i in numbers:
            self.each(i, 0, lambda copy: copy.start())

    def arrived(self, i):
        self.each(i, 1, lambda copy: copy.wait_recv())
        self.start(*self.then.get(i, ()))

    def sent(self):
        for i in range(len(COPIES)):
            self.each(i, 0, lambda copy: copy.wait_send())


def kernel(pattern_hbm, y_hbm, out_ref, pattern, rows, cols, squares, total, local, send, recv, pair_send, pair_recv):
    row = lax.axis_index("row")
    col = lax.axis_index("col")
    x, z_hi = lax.rem(row, 4), row // 4
    y, z_lo, core = col // 4, lax.rem(col // 2, 2), lax.rem(col, 2)

    def in_row(y_, z_):
        return row, y_ * 4 + z_ * 2 + core

    def in_col(x_, z_):
        return z_ * 4 + x_, col

    def row_place(y_, z_):
        return y_ * 4 + z_ * 2 + core

    def col_place(x_, z_):
        return z_ * 4 + x_

    def row_cell(y_, z_):
        return y_ // 2, lax.rem(y_, 2) * 2 + z_

    def col_cell(x_, z_):
        return z_, x_

    p, q = col_cell(x, z_hi), row_cell(y, z_lo)
    sibling = (row, col + 1 - 2 * core)
    barrier = pltpu.get_barrier_semaphore()
    partners = [sibling, in_row(y, 1 - z_lo), in_col(x, 1 - z_hi)]
    for side in (1, 3):
        partners += [in_row(ring(y + side), z_lo), in_col(ring(x + side), z_hi)]
    for partner in partners:
        pl.semaphore_signal(barrier, inc=1, device_id=partner, device_id_type=MESH)
    loads = [pltpu.make_async_copy(pattern_hbm, pattern, local.at[4])]
    for j in range(2):
        half = y_hbm.at[:, pl.ds(j * BLOCK, BLOCK)]
        loads.append(pltpu.make_async_copy(half, rows.at[0, col, j], local.at[j]))
        loads.append(pltpu.make_async_copy(half, cols.at[0, row, j], local.at[2 + j]))
    for load in loads:
        load.start()
    for load in loads:
        load.wait()
    pl.semaphore_wait(barrier, len(partners))

    def clear(refs, place, cell, fixed, side):
        def wipe(j, low, count):
            for ref in refs:
                for step in range(2):
                    ref[step, place, j, pl.ds(low * BLOCK, count * BLOCK)] = jnp.zeros((count * BLOCK, BLOCK), jnp.bfloat16)

        r = reach(cell, fixed)

        @pl.when(r == -1)
        def _():
            for j in range(2):
                wipe(j, 0, 4)

        def act(width):
            wipe(side, (1 - side) * (width + 1), 3 - width)
            if width == 1:
                wipe(1 - side, (1 - side) * 3, 1)
            if width == 0:
                for low in (0, 2 - side, 3):
                    wipe(1 - side, low, 1)

        when_reach(r, act)
        return wipe

    def clear_all():
        def at_row(s, _):
            clear((rows,), 2 * s + core, row_cell(s // 2, lax.rem(s, 2)), p, core)
            return 0

        def at_col(s, _):
            wipe = clear((cols, squares), s, col_cell(lax.rem(s, 4), s // 4), q, core)
            pl.when(lax.rem(s, 4) + x == 3)(lambda: pl.when(lax.rem(x, 3) == 0)(lambda: wipe(core, 0, 4)))
            return 0

        lax.fori_loop(0, 8, at_row, 0)
        lax.fori_loop(0, 8, at_col, 0)

    def product(left, right, m, places):
        at = pl.ds(pl.multiple_of(m * COLS, COLS), COLS)
        terms = []
        for k in places:
            for c in range(2):
                l = jnp.concatenate([left[2 * k + c, j, at] for j in range(2)], axis=1)
                r = jnp.concatenate([right[k, j, pl.ds(c * COLS, COLS)] for j in range(2)], axis=1)
                terms.append(jnp.dot(l, r, preferred_element_type=F32))
        return sum(terms)

    def masked(m, value, store):
        for i in range(2):
            for j in range(2):
                keep = pattern[row * 4 + 2 * m + i, col * 2 + j].astype(F32)
                at = pl.ds(pl.multiple_of((2 * m + i) * BLOCK, BLOCK), BLOCK)
                store(at, j, keep * value(at, i, j))

    def square_gather(step):
        n = 3 * step + 2
        return Gather(squares.at[step], col_place, in_col, col_cell, q, core, x, z_hi, send.at[n], recv.at[n], SQUARE_KIND, near_centre)

    def one_step(step, _):
        y_rows, y_cols, square = rows.at[step], cols.at[step], squares.at[step]
        n = 3 * step
        by_row = Gather(y_rows, row_place, in_row, row_cell, p, core, y, z_lo, send.at[n], recv.at[n], ROW_KIND, same_halves)
        by_col = Gather(y_cols, col_place, in_col, col_cell, q, core, x, z_hi, send.at[n + 1], recv.at[n + 1], COL_KIND, near_centre)
        by_square = square_gather(step)
        shared = []

        def share(number, y_, z_, side):
            ref = y_rows.at[y_ * 4 + z_ * 2 + (1 - core if side else core)]
            return pltpu.make_async_remote_copy(
                src_ref=ref, dst_ref=ref, send_sem=pair_send.at[step, number], recv_sem=pair_recv.at[step, number],
                device_id=sibling, device_id_type=MESH,
            )

        def share_start(y_, z_):
            share(len(shared), y_, z_, 0).start()
            shared.append((y_, z_))

        gathers = {"r": by_row, "c": by_col}
        for name in OWN:
            gathers[name[0]].start(int(name[1:]))
        pl.when(step == 0)(clear_all)
        share_start(y, z_lo)
        here = set()
        for name in WAITS:
            gathers[name[0]].arrived(int(name[1:]))
            if name[0] == "r":
                here.add(int(name[1:]))
                for parts, (offset, other) in TILES.items():
                    if int(name[1:]) in parts and here.issuperset(parts):
                        share_start(ring(y + offset), 1 - z_lo if other else z_lo)
        pl.when(step == 1)(square_gather(0).sent)
        for number, (y_, z_) in enumerate(shared):
            share(number, y_, z_, 1).wait_recv()
        scale = 1.0 / (3.0 * 4096)

        def square_half(m, _):
            full = product(y_rows, y_cols, m, range(8))

            def store_square(at, j, block):
                square[row, j, at] = block.astype(jnp.bfloat16)

            masked(m, lambda at, i, j: full[i * BLOCK : (i + 1) * BLOCK, j * BLOCK : (j + 1) * BLOCK] * scale, store_square)
            return 0

        lax.fori_loop(0, 2, square_half, 0)
        by_square.start(*SQUARE_OWN)
        for i in SQUARE_WAITS[:8]:
            by_square.arrived(i)
        by_row.sent()
        by_col.sent()
        for number, (y_, z_) in enumerate(shared):
            share(number, y_, z_, 0).wait_send()

        def near_half(m, _):
            total[pl.ds(pl.multiple_of(m * COLS, COLS), COLS)] = product(y_rows, square, m, [z_hi * 4 + k for k in range(4)])
            return 0

        lax.fori_loop(0, 2, near_half, 0)
        for i in SQUARE_WAITS[8:12]:
            by_square.arrived(i)

        def side_half(m, _):
            at = pl.ds(pl.multiple_of(m * COLS, COLS), COLS)
            total[at] += product(y_rows, square, m, [(1 - z_hi) * 4 + ring(x + k) for k in (3, 0, 1)])
            return 0

        lax.fori_loop(0, 2, side_half, 0)
        for i in SQUARE_WAITS[12:]:
            by_square.arrived(i)

        def far_half(m, _):
            full = total[pl.ds(pl.multiple_of(m * COLS, COLS), COLS)]
            full += product(y_rows, square, m, [(1 - z_hi) * 4 + ring(x + 2)])

            def updated(at, i, j):
                cube = full[i * BLOCK : (i + 1) * BLOCK, j * BLOCK : (j + 1) * BLOCK]
                return 1.5 * y_rows[col, j, at].astype(F32) - 0.5 * cube

            def store_next(at, j, block):
                @pl.when(step == 0)
                def _():
                    rows[1, col, j, at] = block.astype(jnp.bfloat16)
                    cols[1, row, j, at] = block.astype(jnp.bfloat16)

                @pl.when(step == 1)
                def _():
                    out_ref[at, pl.ds(j * BLOCK, BLOCK)] = block

            masked(m, updated, store_next)
            return 0

        lax.fori_loop(0, 2, far_half, 0)
        return 0

    lax.fori_loop(0, 2, one_step, 0)
    square_gather(1).sent()


def shards(pattern, matrix):
    return pl.pallas_call(
        kernel,
        name="sign_steps",
        out_shape=pltpu.VMEM((ROWS, COLS), F32),
        in_specs=[pl.BlockSpec(memory_space=pl.ANY)] * 2,
        out_specs=pl.BlockSpec(memory_space=pltpu.VMEM),
        scratch_shapes=[
            pltpu.SMEM((32, 32), jnp.int32),
            pltpu.VMEM((2, 16, 2, ROWS, BLOCK), jnp.bfloat16),
            pltpu.VMEM((2, 8, 2, ROWS, BLOCK), jnp.bfloat16),
            pltpu.VMEM((2, 8, 2, ROWS, BLOCK), jnp.bfloat16),
            pltpu.VMEM((ROWS, COLS), F32),
            pltpu.SemaphoreType.DMA((5,)),
            pltpu.SemaphoreType.DMA((6, len(COPIES))),
            pltpu.SemaphoreType.DMA((6, len(COPIES))),
            pltpu.SemaphoreType.DMA((2, 8)),
            pltpu.SemaphoreType.DMA((2, 8)),
        ],
        compiler_params=pltpu.CompilerParams(collective_id=0, has_side_effects=True, vmem_limit_bytes=40 << 20),
        cost_estimate=pl.CostEstimate(flops=4 * 2 * 512 * 256 * 4096, bytes_accessed=1 << 20, transcendentals=0),
    )(*(pltpu.with_memory_space_constraint(a, pltpu.HBM) for a in (pattern, matrix)))


def solution(mesh):
    in_specs = (P(), P("row", "col"))
    return jax.shard_map(shards, mesh=mesh, in_specs=in_specs, out_specs=P("row", "col"), check_vma=False)
```

```python
import jax
import jax.numpy as jnp
from jax import lax
from jax.experimental import pallas as pl
from jax.experimental.pallas import tpu as pltpu
from jax.sharding import PartitionSpec as P

MESH = pl.DeviceIdType.MESH
BLOCK = 128
ROWS, COLS = 512, 256
RING = 4
F32 = jnp.float32

COPIES = (
    ("up", 1, 0, 0), ("not up", 1, 0, 0), ("not down", -1, 0, 0), ("down", -1, 0, 0), ("up", 0, 0, 0), ("not up", 0, 0, 0),
    ("relay", 1, -1, 0), ("relay down", -1, 1, 0),
    ("up", 1, 0, 1), ("not up", 1, 0, 1), ("not down", -1, 0, 1), ("down", -1, 0, 1),
    ("relay", 1, -1, 1), ("relay down", -1, 1, 1),
)
ACROSS = COPIES[:12] + (("far", 0, 2, 0), ("not far", 0, 2, 0))
SECOND = (1, 2, 9, 10)


def same_halves(me, half):
    return half in ("up", "not down", "relay", "far")


def near_centre(me, half):
    return {
        "up": me < 2, "not up": me >= 2, "down": me >= 2, "not down": me < 2, "relay": (me + 1) // 2 == 1,
        "relay down": (me + 1) // 2 == 1, "far": me >= 2, "not far": me < 2,
    }[half]


AROUND = (COPIES, {0: (6,), 3: (7,), 4: (8,), 5: (11, 9, 10), 8: (12,), 11: (13,)})
OVER = (ACROSS, {0: (6,), 3: (7,), 4: (8, 10), 5: (11, 9), 6: (12,), 7: (13,)})
TILES = {(0, 1): (-1, 0), (2, 3): (1, 0), (4, 5): (0, 1), (6, 7): (2, 0), (8, 9): (-1, 1), (10, 11): (1, 1), (12, 13): (2, 1)}
OWN = ("c4", "r3", "c0", "r0", "c3", "c5", "c1", "r1", "c2", "r2", "r4", "r5")
WAITS = (
    "r0", "c0", "r3", "c3", "c4", "c5", "r1", "r2", "r6", "r7", "r4", "c8", "c11", "r5",
    "r8", "r9", "r10", "r11", "r12", "r13", "c1", "c2", "c6", "c7", "c9", "c10", "c12", "c13",
)
SQUARE_OWN = (4, 0, 3, 5, 1, 2)
SQUARE_WAITS = (0, 3, 4, 5, 6, 7, 1, 2, 8, 9, 10, 11, 12, 13)
ROW_KIND, COL_KIND, SQUARE_KIND = OVER, AROUND, OVER


def ring(i):
    return lax.rem(i + RING, RING)


def reach(cell, other):
    dx = lax.max(cell[0] - other[0], other[0] - cell[0])
    dy = lax.max(cell[1] - other[1], other[1] - cell[1])
    return jnp.where(dy == 3, -1, lax.min(2, 3 - dx - dy))


def run(width, inner, core):
    if not inner:
        return core * (3 - width), width + 1
    return ((core + 1, 1), (core, 3), (0, 4))[width]


def when_reach(r, action):
    for width in range(3):
        pl.when(r == width)(lambda width=width: action(width))


class Gather:
    def __init__(self, buf, place, device, cell, fixed, core, me, plane, send, recv, kind, halves):
        self.copies, self.then = kind
        self.halves = halves
        self.buf, self.place, self.device, self.cell = buf, place, device, cell
        self.fixed, self.core, self.me, self.plane = fixed, core, me, plane
        self.send, self.recv = send, recv

    def each(self, i, arriving, action):
        half, side, offset, other = self.copies[i]
        sender = ring(self.me - side) if arriving and side else self.me
        plane = 1 - self.plane if arriving and not side else self.plane
        owner = (ring(sender + offset), 1 - plane if other else plane)
        target = (ring(self.me + side), self.plane if side else 1 - self.plane)
        outer = self.halves(sender, half)
        r = reach(self.cell(*owner), self.fixed)
        if self.halves is near_centre and i in SECOND:
            r = jnp.where(sender == (3 if side > 0 else 0), -1, r)

        def act(width, inner):
            low, count = run(width, inner, self.core)
            j = 1 - self.core if inner else self.core
            ref = self.buf.at[self.place(*owner), j, pl.ds(low * BLOCK, count * BLOCK)]
            action(pltpu.make_async_remote_copy(
                src_ref=ref, dst_ref=ref, send_sem=self.send.at[i], recv_sem=self.recv.at[i],
                device_id=self.device(*target), device_id_type=MESH,
            ))

        if isinstance(outer, bool):
            when_reach(r, lambda width: act(width, not outer))
        else:
            code = r * 2 + jnp.where(outer, 0, 1)
            for width in range(3):
                for inner in (False, True):
                    pl.when(code == 2 * width + inner)(lambda width=width, inner=inner: act(width, inner))

    def start(self, *numbers):
        for i in numbers:
            self.each(i, 0, lambda copy: copy.start())

    def arrived(self, i):
        self.each(i, 1, lambda copy: copy.wait_recv())
        self.start(*self.then.get(i, ()))

    def sent(self):
        for i in range(len(COPIES)):
            self.each(i, 0, lambda copy: copy.wait_send())


def kernel(pattern_hbm, y_hbm, out_ref, pattern, rows, cols, squares, total, local, send, recv, pair_send, pair_recv):
    row = lax.axis_index("row")
    col = lax.axis_index("col")
    x, z_hi = lax.rem(row, 4), row // 4
    y, z_lo, core = col // 4, lax.rem(col // 2, 2), lax.rem(col, 2)

    def in_row(y_, z_):
        return row, y_ * 4 + z_ * 2 + core

    def in_col(x_, z_):
        return z_ * 4 + x_, col

    def row_place(y_, z_):
        return y_ * 4 + z_ * 2 + core

    def col_place(x_, z_):
        return z_ * 4 + x_

    def row_cell(y_, z_):
        return y_ // 2, lax.rem(y_, 2) * 2 + z_

    def col_cell(x_, z_):
        return z_, x_

    p, q = col_cell(x, z_hi), row_cell(y, z_lo)
    sibling = (row, col + 1 - 2 * core)
    barrier = pltpu.get_barrier_semaphore()
    partners = [sibling, in_row(y, 1 - z_lo), in_col(x, 1 - z_hi)]
    for side in (1, 3):
        partners += [in_row(ring(y + side), z_lo), in_col(ring(x + side), z_hi)]
    for partner in partners:
        pl.semaphore_signal(barrier, inc=1, device_id=partner, device_id_type=MESH)
    loads = [pltpu.make_async_copy(pattern_hbm, pattern, local.at[4])]
    for j in range(2):
        half = y_hbm.at[:, pl.ds(j * BLOCK, BLOCK)]
        loads.append(pltpu.make_async_copy(half, rows.at[0, col, j], local.at[j]))
        loads.append(pltpu.make_async_copy(half, cols.at[0, row, j], local.at[2 + j]))
    for load in loads:
        load.start()
    for load in loads:
        load.wait()
    pl.semaphore_wait(barrier, len(partners))

    def clear(refs, place, cell, fixed, side):
        def wipe(j, low, count):
            for ref in refs:
                for step in range(2):
                    ref[step, place, j, pl.ds(low * BLOCK, count * BLOCK)] = jnp.zeros((count * BLOCK, BLOCK), jnp.bfloat16)

        r = reach(cell, fixed)

        @pl.when(r == -1)
        def _():
            for j in range(2):
                wipe(j, 0, 4)

        def act(width):
            wipe(side, (1 - side) * (width + 1), 3 - width)
            if width == 1:
                wipe(1 - side, (1 - side) * 3, 1)
            if width == 0:
                for low in (0, 2 - side, 3):
                    wipe(1 - side, low, 1)

        when_reach(r, act)
        return wipe

    def clear_all():
        def at_row(s, _):
            clear((rows,), 2 * s + core, row_cell(s // 2, lax.rem(s, 2)), p, core)
            return 0

        def at_col(s, _):
            wipe = clear((cols, squares), s, col_cell(lax.rem(s, 4), s // 4), q, core)
            pl.when(lax.rem(s, 4) + x == 3)(lambda: pl.when(lax.rem(x, 3) == 0)(lambda: wipe(core, 0, 4)))
            return 0

        lax.fori_loop(0, 8, at_row, 0)
        lax.fori_loop(0, 8, at_col, 0)

    def product(left, right, m, places):
        at = pl.ds(pl.multiple_of(m * COLS, COLS), COLS)
        terms = []
        for k in places:
            for c in range(2):
                l = jnp.concatenate([left[2 * k + c, j, at] for j in range(2)], axis=1)
                r = jnp.concatenate([right[k, j, pl.ds(c * COLS, COLS)] for j in range(2)], axis=1)
                terms.append(jnp.dot(l, r, preferred_element_type=F32))
        return sum(terms)

    def masked(m, value, store):
        for i in range(2):
            for j in range(2):
                keep = pattern[row * 4 + 2 * m + i, col * 2 + j].astype(F32)
                at = pl.ds(pl.multiple_of((2 * m + i) * BLOCK, BLOCK), BLOCK)
                store(at, j, keep * value(at, i, j))

    def square_gather(step):
        n = 3 * step + 2
        return Gather(squares.at[step], col_place, in_col, col_cell, q, core, x, z_hi, send.at[n], recv.at[n], SQUARE_KIND, near_centre)

    def one_step(step, _):
        y_rows, y_cols, square = rows.at[step], cols.at[step], squares.at[step]
        n = 3 * step
        by_row = Gather(y_rows, row_place, in_row, row_cell, p, core, y, z_lo, send.at[n], recv.at[n], ROW_KIND, same_halves)
        by_col = Gather(y_cols, col_place, in_col, col_cell, q, core, x, z_hi, send.at[n + 1], recv.at[n + 1], COL_KIND, near_centre)
        by_square = square_gather(step)
        shared = []

        def share(number, y_, z_, side):
            ref = y_rows.at[y_ * 4 + z_ * 2 + (1 - core if side else core)]
            return pltpu.make_async_remote_copy(
                src_ref=ref, dst_ref=ref, send_sem=pair_send.at[step, number], recv_sem=pair_recv.at[step, number],
                device_id=sibling, device_id_type=MESH,
            )

        def share_start(y_, z_):
            share(len(shared), y_, z_, 0).start()
            shared.append((y_, z_))

        gathers = {"r": by_row, "c": by_col}
        for name in OWN:
            gathers[name[0]].start(int(name[1:]))
        pl.when(step == 0)(clear_all)
        share_start(y, z_lo)
        here = set()
        for name in WAITS:
            gathers[name[0]].arrived(int(name[1:]))
            if name[0] == "r":
                here.add(int(name[1:]))
                for parts, (offset, other) in TILES.items():
                    if int(name[1:]) in parts and here.issuperset(parts):
                        share_start(ring(y + offset), 1 - z_lo if other else z_lo)
        pl.when(step == 1)(square_gather(0).sent)
        for number, (y_, z_) in enumerate(shared):
            share(number, y_, z_, 1).wait_recv()
        scale = 1.0 / (3.0 * 4096)

        def square_half(m, _):
            full = product(y_rows, y_cols, m, range(8))

            def store_square(at, j, block):
                square[row, j, at] = block.astype(jnp.bfloat16)

            masked(m, lambda at, i, j: full[i * BLOCK : (i + 1) * BLOCK, j * BLOCK : (j + 1) * BLOCK] * scale, store_square)
            return 0

        lax.fori_loop(0, 2, square_half, 0)
        by_square.start(*SQUARE_OWN)
        for i in SQUARE_WAITS[:8]:
            by_square.arrived(i)
        by_row.sent()
        by_col.sent()
        for number, (y_, z_) in enumerate(shared):
            share(number, y_, z_, 0).wait_send()

        def near_half(m, _):
            total[pl.ds(pl.multiple_of(m * COLS, COLS), COLS)] = product(y_rows, square, m, [z_hi * 4 + k for k in range(4)])
            return 0

        lax.fori_loop(0, 2, near_half, 0)
        for i in SQUARE_WAITS[8:12]:
            by_square.arrived(i)

        def side_half(m, _):
            at = pl.ds(pl.multiple_of(m * COLS, COLS), COLS)
            total[at] += product(y_rows, square, m, [(1 - z_hi) * 4 + ring(x + k) for k in (3, 0, 1)])
            return 0

        lax.fori_loop(0, 2, side_half, 0)
        for i in SQUARE_WAITS[12:]:
            by_square.arrived(i)

        def far_half(m, _):
            full = total[pl.ds(pl.multiple_of(m * COLS, COLS), COLS)]
            full += product(y_rows, square, m, [(1 - z_hi) * 4 + ring(x + 2)])

            def updated(at, i, j):
                cube = full[i * BLOCK : (i + 1) * BLOCK, j * BLOCK : (j + 1) * BLOCK]
                return 1.5 * y_rows[col, j, at].astype(F32) - 0.5 * cube

            def store_next(at, j, block):
                @pl.when(step == 0)
                def _():
                    rows[1, col, j, at] = block.astype(jnp.bfloat16)
                    cols[1, row, j, at] = block.astype(jnp.bfloat16)

                @pl.when(step == 1)
                def _():
                    out_ref[at, pl.ds(j * BLOCK, BLOCK)] = block

            masked(m, updated, store_next)
            return 0

        lax.fori_loop(0, 2, far_half, 0)
        return 0

    lax.fori_loop(0, 2, one_step, 0)
    square_gather(1).sent()


def shards(pattern, matrix):
    return pl.pallas_call(
        kernel,
        name="sign_steps",
        out_shape=pltpu.VMEM((ROWS, COLS), F32),
        in_specs=[pl.BlockSpec(memory_space=pl.ANY)] * 2,
        out_specs=pl.BlockSpec(memory_space=pltpu.VMEM),
        scratch_shapes=[
            pltpu.SMEM((32, 32), jnp.int32),
            pltpu.VMEM((2, 16, 2, ROWS, BLOCK), jnp.bfloat16),
            pltpu.VMEM((2, 8, 2, ROWS, BLOCK), jnp.bfloat16),
            pltpu.VMEM((2, 8, 2, ROWS, BLOCK), jnp.bfloat16),
            pltpu.VMEM((ROWS, COLS), F32),
            pltpu.SemaphoreType.DMA((5,)),
            pltpu.SemaphoreType.DMA((6, len(COPIES))),
            pltpu.SemaphoreType.DMA((6, len(COPIES))),
            pltpu.SemaphoreType.DMA((2, 8)),
            pltpu.SemaphoreType.DMA((2, 8)),
        ],
        compiler_params=pltpu.CompilerParams(collective_id=0, has_side_effects=True, vmem_limit_bytes=40 << 20),
        cost_estimate=pl.CostEstimate(flops=4 * 2 * 512 * 256 * 4096, bytes_accessed=1 << 20, transcendentals=0),
    )(*(pltpu.with_memory_space_constraint(a, pltpu.HBM) for a in (pattern, matrix)))


def solution(mesh):
    in_specs = (P(), P("row", "col"))
    return jax.shard_map(shards, mesh=mesh, in_specs=in_specs, out_specs=P("row", "col"), check_vma=False)
```

```python
import jax
import jax.numpy as jnp
from jax import lax
from jax.experimental import pallas as pl
from jax.experimental.pallas import tpu as pltpu
from jax.sharding import PartitionSpec as P

MESH = pl.DeviceIdType.MESH
BLOCK = 128
ROWS, COLS = 512, 256
RING = 4
F32 = jnp.float32

COPIES = (
    ("up", 1, 0, 0), ("not up", 1, 0, 0), ("not down", -1, 0, 0), ("down", -1, 0, 0), ("up", 0, 0, 0), ("not up", 0, 0, 0),
    ("relay", 1, -1, 0), ("relay down", -1, 1, 0),
    ("up", 1, 0, 1), ("not up", 1, 0, 1), ("not down", -1, 0, 1), ("down", -1, 0, 1),
    ("relay", 1, -1, 1), ("relay down", -1, 1, 1),
)
ACROSS = COPIES[:12] + (("far", 0, 2, 0), ("not far", 0, 2, 0))
SECOND = (1, 2, 9, 10)


def same_halves(me, half):
    return half in ("up", "not down", "relay", "far")


def near_centre(me, half):
    return {
        "up": me < 2, "not up": me >= 2, "down": me >= 2, "not down": me < 2, "relay": (me + 1) // 2 == 1,
        "relay down": (me + 1) // 2 == 1, "far": me >= 2, "not far": me < 2,
    }[half]


AROUND = (COPIES, {0: (6,), 3: (7,), 4: (8,), 5: (11, 9, 10), 8: (12,), 11: (13,)})
OVER = (ACROSS, {0: (6,), 3: (7,), 4: (8, 10), 5: (11, 9), 6: (12,), 7: (13,)})
TILES = {(0, 1): (-1, 0), (2, 3): (1, 0), (4, 5): (0, 1), (6, 7): (2, 0), (8, 9): (-1, 1), (10, 11): (1, 1), (12, 13): (2, 1)}
OWN = ("c4", "r3", "c0", "r0", "c3", "c5", "c1", "r1", "c2", "r2", "r4", "r5")
WAITS = (
    "r0", "c0", "r3", "c3", "c4", "c5", "r1", "r2", "r6", "r7", "r4", "c8", "c11", "r5",
    "r8", "r9", "r10", "r11", "r12", "r13", "c1", "c2", "c6", "c7", "c9", "c10", "c12", "c13",
)
SQUARE_OWN = (4, 0, 3, 5, 1, 2)
SQUARE_WAITS = (0, 3, 4, 5, 6, 7, 1, 2, 8, 9, 10, 11, 12, 13)
ROW_KIND, COL_KIND, SQUARE_KIND = OVER, AROUND, OVER


def ring(i):
    return lax.rem(i + RING, RING)


def reach(cell, other):
    dx = lax.max(cell[0] - other[0], other[0] - cell[0])
    dy = lax.max(cell[1] - other[1], other[1] - cell[1])
    return jnp.where(dy == 3, -1, lax.min(2, 3 - dx - dy))


def run(width, inner, core):
    if not inner:
        return core * (3 - width), width + 1
    return ((core + 1, 1), (core, 3), (0, 4))[width]


def when_reach(r, action):
    for width in range(3):
        pl.when(r == width)(lambda width=width: action(width))


class Gather:
    def __init__(self, buf, place, device, cell, fixed, core, me, plane, send, recv, kind, halves):
        self.copies, self.then = kind
        self.halves = halves
        self.buf, self.place, self.device, self.cell = buf, place, device, cell
        self.fixed, self.core, self.me, self.plane = fixed, core, me, plane
        self.send, self.recv = send, recv

    def each(self, i, arriving, action):
        half, side, offset, other = self.copies[i]
        sender = ring(self.me - side) if arriving and side else self.me
        plane = 1 - self.plane if arriving and not side else self.plane
        owner = (ring(sender + offset), 1 - plane if other else plane)
        target = (ring(self.me + side), self.plane if side else 1 - self.plane)
        outer = self.halves(sender, half)
        r = reach(self.cell(*owner), self.fixed)
        if self.halves is near_centre and i in SECOND:
            r = jnp.where(sender == (3 if side > 0 else 0), -1, r)

        if self.halves is same_halves and 8 <= i < 12:
            r = jnp.where(lax.rem(sender + plane, 2) == 1, -1, r)

        def act(width, inner):
            low, count = run(width, inner, self.core)
            j = 1 - self.core if inner else self.core
            ref = self.buf.at[self.place(*owner), j, pl.ds(low * BLOCK, count * BLOCK)]
            action(pltpu.make_async_remote_copy(
                src_ref=ref, dst_ref=ref, send_sem=self.send.at[i], recv_sem=self.recv.at[i],
                device_id=self.device(*target), device_id_type=MESH,
            ))

        if isinstance(outer, bool):
            when_reach(r, lambda width: act(width, not outer))
        else:
            code = r * 2 + jnp.where(outer, 0, 1)
            for width in range(3):
                for inner in (False, True):
                    pl.when(code == 2 * width + inner)(lambda width=width, inner=inner: act(width, inner))

    def start(self, *numbers):
        for i in numbers:
            self.each(i, 0, lambda copy: copy.start())

    def arrived(self, i):
        self.each(i, 1, lambda copy: copy.wait_recv())
        self.start(*self.then.get(i, ()))

    def sent(self):
        for i in range(len(COPIES)):
            self.each(i, 0, lambda copy: copy.wait_send())


def kernel(pattern_hbm, y_hbm, out_ref, pattern, rows, cols, squares, total, local, send, recv, pair_send, pair_recv):
    row = lax.axis_index("row")
    col = lax.axis_index("col")
    x, z_hi = lax.rem(row, 4), row // 4
    y, z_lo, core = col // 4, lax.rem(col // 2, 2), lax.rem(col, 2)

    def in_row(y_, z_):
        return row, y_ * 4 + z_ * 2 + core

    def in_col(x_, z_):
        return z_ * 4 + x_, col

    def row_place(y_, z_):
        return y_ * 4 + z_ * 2 + core

    def col_place(x_, z_):
        return z_ * 4 + x_

    def row_cell(y_, z_):
        return y_ // 2, lax.rem(y_, 2) * 2 + z_

    def col_cell(x_, z_):
        return z_, x_

    p, q = col_cell(x, z_hi), row_cell(y, z_lo)
    sibling = (row, col + 1 - 2 * core)
    barrier = pltpu.get_barrier_semaphore()
    partners = [sibling, in_row(y, 1 - z_lo), in_col(x, 1 - z_hi)]
    for side in (1, 3):
        partners += [in_row(ring(y + side), z_lo), in_col(ring(x + side), z_hi)]
    for partner in partners:
        pl.semaphore_signal(barrier, inc=1, device_id=partner, device_id_type=MESH)
    loads = [pltpu.make_async_copy(pattern_hbm, pattern, local.at[4])]
    for j in range(2):
        half = y_hbm.at[:, pl.ds(j * BLOCK, BLOCK)]
        loads.append(pltpu.make_async_copy(half, rows.at[0, col, j], local.at[j]))
        loads.append(pltpu.make_async_copy(half, cols.at[0, row, j], local.at[2 + j]))
    for load in loads:
        load.start()
    for load in loads:
        load.wait()
    pl.semaphore_wait(barrier, len(partners))

    def clear(refs, place, cell, fixed, side):
        def wipe(j, low, count):
            for ref in refs:
                for step in range(2):
                    ref[step, place, j, pl.ds(low * BLOCK, count * BLOCK)] = jnp.zeros((count * BLOCK, BLOCK), jnp.bfloat16)

        r = reach(cell, fixed)

        @pl.when(r == -1)
        def _():
            for j in range(2):
                wipe(j, 0, 4)

        def act(width):
            wipe(side, (1 - side) * (width + 1), 3 - width)
            if width == 1:
                wipe(1 - side, (1 - side) * 3, 1)
            if width == 0:
                for low in (0, 2 - side, 3):
                    wipe(1 - side, low, 1)

        when_reach(r, act)
        return wipe

    def clear_all():
        def at_row(s, _):
            wipe = clear((rows,), 2 * s + core, row_cell(s // 2, lax.rem(s, 2)), p, core)
            apart = lax.rem(s // 2 + y, 2) * lax.rem(s + z_lo, 2) * lax.rem(s // 2 + z_lo, 2)
            pl.when(apart == 1)(lambda: [wipe(j, 0, 4) for j in range(2)] and None)
            return 0

        def at_col(s, _):
            wipe = clear((cols, squares), s, col_cell(lax.rem(s, 4), s // 4), q, core)
            pl.when(lax.rem(s, 4) + x == 3)(lambda: pl.when(lax.rem(x, 3) == 0)(lambda: wipe(core, 0, 4)))
            return 0

        lax.fori_loop(0, 8, at_row, 0)
        lax.fori_loop(0, 8, at_col, 0)

    def product(left, right, m, places):
        at = pl.ds(pl.multiple_of(m * COLS, COLS), COLS)
        terms = []
        for k in places:
            for c in range(2):
                l = jnp.concatenate([left[2 * k + c, j, at] for j in range(2)], axis=1)
                r = jnp.concatenate([right[k, j, pl.ds(c * COLS, COLS)] for j in range(2)], axis=1)
                terms.append(jnp.dot(l, r, preferred_element_type=F32))
        return sum(terms)

    def masked(m, value, store):
        for i in range(2):
            for j in range(2):
                keep = pattern[row * 4 + 2 * m + i, col * 2 + j].astype(F32)
                at = pl.ds(pl.multiple_of((2 * m + i) * BLOCK, BLOCK), BLOCK)
                store(at, j, keep * value(at, i, j))

    def square_gather(step):
        n = 3 * step + 2
        return Gather(squares.at[step], col_place, in_col, col_cell, q, core, x, z_hi, send.at[n], recv.at[n], SQUARE_KIND, near_centre)

    def one_step(step, _):
        y_rows, y_cols, square = rows.at[step], cols.at[step], squares.at[step]
        n = 3 * step
        by_row = Gather(y_rows, row_place, in_row, row_cell, p, core, y, z_lo, send.at[n], recv.at[n], ROW_KIND, same_halves)
        by_col = Gather(y_cols, col_place, in_col, col_cell, q, core, x, z_hi, send.at[n + 1], recv.at[n + 1], COL_KIND, near_centre)
        by_square = square_gather(step)
        shared = []

        def share(number, y_, z_, side):
            ref = y_rows.at[y_ * 4 + z_ * 2 + (1 - core if side else core)]
            return pltpu.make_async_remote_copy(
                src_ref=ref, dst_ref=ref, send_sem=pair_send.at[step, number], recv_sem=pair_recv.at[step, number],
                device_id=sibling, device_id_type=MESH,
            )

        def share_start(y_, z_):
            share(len(shared), y_, z_, 0).start()
            shared.append((y_, z_))

        gathers = {"r": by_row, "c": by_col}
        for name in OWN:
            gathers[name[0]].start(int(name[1:]))
        pl.when(step == 0)(clear_all)
        share_start(y, z_lo)
        pl.when(step == 1)(square_gather(0).sent)
        here = set()
        for name in WAITS:
            gathers[name[0]].arrived(int(name[1:]))
            if name[0] == "r":
                here.add(int(name[1:]))
                for parts, (offset, other) in TILES.items():
                    if int(name[1:]) in parts and here.issuperset(parts):
                        share_start(ring(y + offset), 1 - z_lo if other else z_lo)
        for number, (y_, z_) in enumerate(shared):
            share(number, y_, z_, 1).wait_recv()
        scale = 1.0 / (3.0 * 4096)

        def square_half(m, _):
            full = product(y_rows, y_cols, m, range(8))

            def store_square(at, j, block):
                square[row, j, at] = block.astype(jnp.bfloat16)

            masked(m, lambda at, i, j: full[i * BLOCK : (i + 1) * BLOCK, j * BLOCK : (j + 1) * BLOCK] * scale, store_square)
            return 0

        lax.fori_loop(0, 2, square_half, 0)
        by_square.start(*SQUARE_OWN)
        for i in SQUARE_WAITS[:8]:
            by_square.arrived(i)
        by_row.sent()
        by_col.sent()
        for number, (y_, z_) in enumerate(shared):
            share(number, y_, z_, 0).wait_send()

        def near_half(m, _):
            total[pl.ds(pl.multiple_of(m * COLS, COLS), COLS)] = product(y_rows, square, m, [z_hi * 4 + k for k in range(4)])
            return 0

        lax.fori_loop(0, 2, near_half, 0)
        for i in SQUARE_WAITS[8:12]:
            by_square.arrived(i)

        def side_half(m, _):
            at = pl.ds(pl.multiple_of(m * COLS, COLS), COLS)
            total[at] += product(y_rows, square, m, [(1 - z_hi) * 4 + ring(x + k) for k in (3, 0, 1)])
            return 0

        lax.fori_loop(0, 2, side_half, 0)
        for i in SQUARE_WAITS[12:]:
            by_square.arrived(i)

        def far_half(m, _):
            full = total[pl.ds(pl.multiple_of(m * COLS, COLS), COLS)]
            full += product(y_rows, square, m, [(1 - z_hi) * 4 + ring(x + 2)])

            def updated(at, i, j):
                cube = full[i * BLOCK : (i + 1) * BLOCK, j * BLOCK : (j + 1) * BLOCK]
                return 1.5 * y_rows[col, j, at].astype(F32) - 0.5 * cube

            def store_next(at, j, block):
                @pl.when(step == 0)
                def _():
                    rows[1, col, j, at] = block.astype(jnp.bfloat16)
                    cols[1, row, j, at] = block.astype(jnp.bfloat16)

                @pl.when(step == 1)
                def _():
                    out_ref[at, pl.ds(j * BLOCK, BLOCK)] = block

            masked(m, updated, store_next)
            return 0

        lax.fori_loop(0, 2, far_half, 0)
        return 0

    lax.fori_loop(0, 2, one_step, 0)
    square_gather(1).sent()


def shards(pattern, matrix):
    return pl.pallas_call(
        kernel,
        name="sign_steps",
        out_shape=pltpu.VMEM((ROWS, COLS), F32),
        in_specs=[pl.BlockSpec(memory_space=pl.ANY)] * 2,
        out_specs=pl.BlockSpec(memory_space=pltpu.VMEM),
        scratch_shapes=[
            pltpu.SMEM((32, 32), jnp.int32),
            pltpu.VMEM((2, 16, 2, ROWS, BLOCK), jnp.bfloat16),
            pltpu.VMEM((2, 8, 2, ROWS, BLOCK), jnp.bfloat16),
            pltpu.VMEM((2, 8, 2, ROWS, BLOCK), jnp.bfloat16),
            pltpu.VMEM((ROWS, COLS), F32),
            pltpu.SemaphoreType.DMA((5,)),
            pltpu.SemaphoreType.DMA((6, len(COPIES))),
            pltpu.SemaphoreType.DMA((6, len(COPIES))),
            pltpu.SemaphoreType.DMA((2, 8)),
            pltpu.SemaphoreType.DMA((2, 8)),
        ],
        compiler_params=pltpu.CompilerParams(collective_id=0, has_side_effects=True, vmem_limit_bytes=40 << 20),
        cost_estimate=pl.CostEstimate(flops=4 * 2 * 512 * 256 * 4096, bytes_accessed=1 << 20, transcendentals=0),
    )(*(pltpu.with_memory_space_constraint(a, pltpu.HBM) for a in (pattern, matrix)))


def solution(mesh):
    in_specs = (P(), P("row", "col"))
    return jax.shard_map(shards, mesh=mesh, in_specs=in_specs, out_specs=P("row", "col"), check_vma=False)
```
